256 devices in a mesh: slab: 4 (over y), inner: 64 (over x, z, core).
Axes of the slice: x: 4, y: 4, z: 8, core: 2. Of those that a mesh axis runs over, the one named last changes fastest.
Arguments:
- expression: float32 [16384, 4096], P('slab', 'inner'), may hold values from -6 to 6
- cell_tiles: bfloat16 [64, 3, 256, 256], P('slab'), may hold values from -0.109375 to 0.109375
- cell_blocks: int32 [64, 3], P('slab'), may hold values from 0 to 63, as said below
- cell_counts: int32 [64], P('slab'), may hold values from 2 to 3, as said below
- gene_tiles: bfloat16 [32, 3, 128, 128], replicated, may hold values from -0.15625 to 0.15625
- gene_blocks: int32 [32, 3], replicated, may hold values from 0 to 31
Outputs:
- lowrank: float32 [16384, 4096], P('slab', 'inner')
The draws below stay inside these ranges and needn't reach their ends.
Inputs may be any that keep to these rules, and one draw needn't show every extreme that they name: `cell_blocks`: row block b lists b first, then b - 1 (1 for b = 0), then a block at most 2 above b (below b when that passes the last block). `cell_counts`: each cell row block uses its first 2 or 3 listed tiles.
All inputs are finite; a program needn't handle non-finite values.
Results may differ from the reference program's by a relative error of at most 0.002.
Values may be sent and summed in bfloat16 or wider, within the bound.
No kernel may reach another device: no remote copies, remote signals or barrier semaphores. Data moves between devices by JAX's collectives and lax.ppermute only.
A program may use at most 128 MiB of HBM per device.

```python
import jax
import jax.numpy as jnp
from jax import lax

GENES = 4096
CT = 256
GT = 128
KC = 3
KG = 3
REACH = 2
STEPS = 2
CELLS = 16384
NB = 64
GB = 32


def draw_cell_blocks(key, part):
    index = jnp.arange(NB, dtype=jnp.int32)
    upward = jax.random.randint(jax.random.fold_in(key, 11), (NB,), 1, REACH + 1).astype(jnp.int32)
    below = jnp.where(index > 0, index - 1, 1)
    above = jnp.where(index + upward <= NB - 1, index + upward, index - upward)
    return jnp.stack([index, below, above], axis=1).astype(jnp.int32)


def draw_cell_counts(key, part):
    index = jnp.arange(NB, dtype=jnp.int32)
    counts = jax.random.randint(jax.random.fold_in(key, 23), (NB,), 2, KC + 1).astype(jnp.int32)
    counts = jnp.where(index % 4 == 0, KC, counts)
    counts = jnp.where(index % 4 == 1, 2, counts)
    return counts.astype(jnp.int32)


def with_ends(values, key, least, largest):
    longest = values.shape.index(max(values.shape))
    spots = []
    for shift in (0, 1):
        where = [jax.random.randint(jax.random.fold_in(key, axis), (), 0, length) for axis, length in enumerate(values.shape)]
        where[longest] = (where[longest] + shift) % values.shape[longest]
        spots.append(tuple(where))
    return values.at[spots[0]].set(least).at[spots[1]].set(largest)


def block_scale(rng, extent, cuts, least, top_value):
    level = 1.0
    for dim, shards_of in cuts:
        draws = jax.random.uniform(jax.random.fold_in(jax.random.fold_in(rng, 6), dim), (shards_of,), jnp.float32, least / len(cuts), top_value / len(cuts))
        level = level * jnp.repeat(jnp.exp(draws), extent[dim] // shards_of).reshape((-1,) + (1,) * (len(extent) - 1 - dim))
    return level


def normal_values(own_key, shape, width, limit, split=(), kind=jnp.bfloat16):
    entries = jax.random.normal(own_key, shape, jnp.float32) * width
    if len(split) > 0:
        entries = block_scale(own_key, shape, split, -0.22, 0.18) * entries
    return jnp.clip(entries, min=-limit, max=limit).astype(kind)


def setup_inputs(seed: int = 0) -> dict:
    key_list = jax.random.split(jax.random.key(seed), 7)
    return {
        "expression": normal_values(key_list[0], (CELLS, GENES), 1.0, 6.0, ((0, 4), (1, 64)), jnp.float32),
        "cell_tiles": normal_values(key_list[1], (NB, KC, CT, CT), (4 * CT * KC) ** -0.5, 0.109375, ((0, 4),)),
        "cell_blocks": draw_cell_blocks(jax.random.fold_in(key_list[6], 71), 0),
        "cell_counts": draw_cell_counts(jax.random.fold_in(key_list[6], 71), 0),
        "gene_tiles": normal_values(key_list[4], (GB, KG, GT, GT), (4 * GT * KG) ** -0.5, 0.15625),
        "gene_blocks": with_ends(jax.random.randint(key_list[5], (GB, KG), 0, GB), jax.random.fold_in(key_list[5], 1), 0, GB - 1).astype(jnp.int32),
    }


shrink = 0.5


def cell_term(lowp, cell_tiles, cell_blocks, cell_counts):
    stacked = lowp.reshape(NB, CT, GENES)

    def one_block(inputs):
        tiles, blocks, count = inputs
        total = jnp.zeros((CT, GENES), jnp.float32)
        for slot in range(KC):
            weight = jnp.where(slot < count, 1.0, 0.0).astype(jnp.float32)
            source = jnp.take(stacked, blocks[slot], axis=0)
            total = total + weight * jnp.dot(tiles[slot], source, preferred_element_type=jnp.float32)
        return total

    return lax.map(one_block, (cell_tiles, cell_blocks, cell_counts)).reshape(NB * CT, GENES)


def gene_term(lowp, gene_tiles, gene_blocks):
    stacked = lowp.reshape(CELLS, GB, GT)

    def one_block(inputs):
        tiles, blocks = inputs
        total = jnp.zeros((CELLS, GT), jnp.float32)
        for slot in range(KG):
            source = jnp.take(stacked, blocks[slot], axis=1)
            total = total + jnp.dot(source, tiles[slot], preferred_element_type=jnp.float32)
        return total

    pieces = lax.map(one_block, (gene_tiles, gene_blocks))
    return jnp.transpose(pieces, (1, 0, 2)).reshape(CELLS, GENES)


def reference(expression, cell_tiles, cell_blocks, cell_counts, gene_tiles, gene_blocks):
    current = expression
    for step in range(STEPS):
        lowp = current.astype(jnp.bfloat16)
        moved = current - (cell_term(lowp, cell_tiles, cell_blocks, cell_counts) + gene_term(lowp, gene_tiles, gene_blocks))
        offset = moved - expression
        current = expression + jnp.sign(offset) * jnp.maximum(jnp.abs(offset) - shrink, 0.0)
    return current
```

```python
import jax
import jax.numpy as jnp
from jax import lax
from jax.experimental import pallas as pl
from jax.experimental.pallas import tpu as pltpu
from jax.sharding import Mesh
from jax.sharding import PartitionSpec as P

CHIPS = 32
OWN = 64
CHUNK = 128
BLOCKS = 16
CT = 256
GB = 32
GT = 128
SLOTS = 3
BEFORE, AFTER = 1, 2
HALF = 0.5

VMEM = pl.BlockSpec(memory_space=pltpu.VMEM)
SMEM = pl.BlockSpec(memory_space=pltpu.SMEM)
CHUNKED = (CHIPS, OWN, CHUNK)
DIMS_NT = (((1,), (1,)), ((), ()))


def soft(v):
    return v - jnp.clip(v, -HALF, HALF)


def params(mib):
    return pltpu.CompilerParams(vmem_limit_bytes=mib << 20)


def cost(flops, moved):
    return pl.CostEstimate(flops=flops, bytes_accessed=moved, transcendentals=0)


def cast_kernel(x_ref, low_ref):
    for j in range(CHIPS):
        low_ref[j] = x_ref[:, j * CHUNK : (j + 1) * CHUNK].astype(jnp.bfloat16)


def cast_chunks(x):
    return pl.pallas_call(
        cast_kernel,
        out_shape=jax.ShapeDtypeStruct(CHUNKED, jnp.bfloat16),
        in_specs=[VMEM],
        out_specs=VMEM,
        compiler_params=params(8),
        cost_estimate=cost(1 << 18, 3 << 19),
        name="cast_chunks",
    )(x)


def step_kernel(x_ref, d_ref, low_ref):
    for j in range(CHIPS):
        moved = x_ref[:, j * CHUNK : (j + 1) * CHUNK] - d_ref[j].astype(jnp.float32)
        low_ref[j] = moved.astype(jnp.bfloat16)


def step_chunks(x, d):
    return pl.pallas_call(
        step_kernel,
        out_shape=jax.ShapeDtypeStruct(CHUNKED, jnp.bfloat16),
        in_specs=[VMEM, VMEM],
        out_specs=VMEM,
        compiler_params=params(8),
        cost_estimate=cost(1 << 18, 2 << 20),
        name="step_chunks",
    )(x, d)


CELL_STEP = 4


def cell_kernel(blocks_ref, counts_ref, before_ref, low_ref, after_ref, tiles_ref, out_ref, all_ref):
    step = pl.program_id(0)
    first = lax.axis_index("slab") * BLOCKS - BEFORE

    @pl.when(step == 0)
    def _():
        all_ref[: 2 * BEFORE] = before_ref[...]
        all_ref[2 * BEFORE : 2 * BEFORE + CHIPS] = low_ref[...]
        all_ref[2 * BEFORE + CHIPS :] = after_ref[...]

    for i in range(CELL_STEP):
        b = step * CELL_STEP + i
        total = jnp.zeros((OWN, CT), jnp.float32)
        for k in range(SLOTS):
            at = 2 * (blocks_ref[k, b] - first)
            source = jnp.concatenate([all_ref[at], all_ref[at + 1]], axis=1)
            part = lax.dot_general(source, tiles_ref[i, k], DIMS_NT, preferred_element_type=jnp.float32)
            used = jnp.where(k < counts_ref[b], 1.0, 0.0).astype(jnp.float32)
            total = total + used * part
        out_ref[2 * i] = total[:, :CHUNK].astype(out_ref.dtype)
        out_ref[2 * i + 1] = total[:, CHUNK:].astype(out_ref.dtype)


def cell_product(blocks, counts, before, low, after, tiles, dtype):
    return pl.pallas_call(
        cell_kernel,
        grid=(BLOCKS // CELL_STEP,),
        out_shape=jax.ShapeDtypeStruct(CHUNKED, dtype),
        in_specs=[
            SMEM,
            SMEM,
            VMEM,
            VMEM,
            VMEM,
            pl.BlockSpec((CELL_STEP, SLOTS, CT, CT), lambda s: (s, 0, 0, 0)),
        ],
        out_specs=pl.BlockSpec((2 * CELL_STEP, OWN, CHUNK), lambda s: (s, 0, 0)),
        scratch_shapes=[pltpu.VMEM((CHIPS + 2 * (BEFORE + AFTER), OWN, CHUNK), jnp.bfloat16)],
        compiler_params=params(16),
        cost_estimate=cost(2 * BLOCKS * SLOTS * CT * CT * OWN, 9 << 20),
        name="cell_product",
    )(blocks, counts, before, low, after, tiles)


TURN_STEP = 8


def turn_kernel(tiles_ref, out_ref):
    low = lax.axis_index("core") == 0
    for i in range(TURN_STEP):
        for k in range(SLOTS):
            t = tiles_ref[i, k].astype(jnp.float32)
            top, bottom = t[:OWN], t[OWN:]
            mine = jnp.where(low, top, bottom)
            other = jnp.where(low, bottom, top)
            turned = jnp.concatenate([mine, other], axis=0).T
            kept = jnp.where(low, turned[:OWN], turned[OWN:])
            out_ref[i, :, k * GT : (k + 1) * GT] = kept.astype(jnp.bfloat16)


def turn_tiles(gene_tiles):
    return pl.pallas_call(
        turn_kernel,
        grid=(GB // TURN_STEP,),
        out_shape=jax.ShapeDtypeStruct((GB, OWN, SLOTS * GT), jnp.bfloat16),
        in_specs=[pl.BlockSpec((TURN_STEP, SLOTS, GT, GT), lambda s: (s, 0, 0, 0))],
        out_specs=pl.BlockSpec((TURN_STEP, OWN, SLOTS * GT), lambda s: (s, 0, 0)),
        compiler_params=params(8),
        cost_estimate=cost(1 << 24, 5 << 20),
        name="turn_tiles",
    )(gene_tiles)


def gene_block(blocks_ref, turned_ref, mine_ref, other_ref, a):
    parts = []
    for k in range(SLOTS):
        at = blocks_ref[k, a]
        parts += [mine_ref[at], other_ref[at]]
    return jnp.dot(turned_ref[a], jnp.concatenate(parts, axis=0), preferred_element_type=jnp.float32)


def gene_kernel(blocks_ref, turned_ref, mine_ref, other_ref, cell_ref, d_ref, low_ref, rest_ref):
    for a in range(GB):
        gene = gene_block(blocks_ref, turned_ref, mine_ref, other_ref, a)
        d = soft(cell_ref[a].astype(jnp.float32) + gene)
        sent = d.astype(jnp.bfloat16)
        d_ref[a] = sent
        rest_ref[a] = d - sent.astype(jnp.float32)
        low_ref[a] = (mine_ref[a].astype(jnp.float32) - d).astype(jnp.bfloat16)


def first_gene_step(blocks, turned, mine, other, cell):
    return pl.pallas_call(
        gene_kernel,
        out_shape=[
            jax.ShapeDtypeStruct(CHUNKED, jnp.bfloat16),
            jax.ShapeDtypeStruct(CHUNKED, jnp.bfloat16),
            jax.ShapeDtypeStruct(CHUNKED, jnp.float32),
        ],
        in_specs=[SMEM, VMEM, VMEM, VMEM, VMEM],
        out_specs=[VMEM, VMEM, VMEM],
        compiler_params=params(16),
        cost_estimate=cost(2 * GB * OWN * SLOTS * GT * CHUNK, 5 << 20),
        name="first_gene_step",
    )(blocks, turned, mine, other, cell)


def second_kernel(blocks_ref, turned_ref, mine_ref, other_ref, rest_ref, out_ref):
    for a in range(GB):
        gene = gene_block(blocks_ref, turned_ref, mine_ref, other_ref, a)
        out_ref[a] = (gene + rest_ref[a]).astype(jnp.bfloat16)


def second_gene_step(blocks, turned, mine, other, rest):
    return pl.pallas_call(
        second_kernel,
        out_shape=jax.ShapeDtypeStruct(CHUNKED, jnp.bfloat16),
        in_specs=[SMEM, VMEM, VMEM, VMEM, VMEM],
        out_specs=VMEM,
        compiler_params=params(16),
        cost_estimate=cost(2 * GB * OWN * SLOTS * GT * CHUNK, 5 << 20),
        name="second_gene_step",
    )(blocks, turned, mine, other, rest)


def last_kernel(x_ref, d_ref, gene_ref, cell_ref, out_ref):
    for j in range(CHIPS):
        v = cell_ref[j] + (d_ref[j].astype(jnp.float32) + gene_ref[j].astype(jnp.float32))
        at = slice(j * CHUNK, (j + 1) * CHUNK)
        out_ref[:, at] = x_ref[:, at] - soft(v)


def last_step(x, d, gene, cell):
    return pl.pallas_call(
        last_kernel,
        out_shape=jax.ShapeDtypeStruct(x.shape, jnp.float32),
        in_specs=[VMEM] * 4,
        out_specs=VMEM,
        compiler_params=params(12),
        cost_estimate=cost(1 << 20, 4 << 20),
        name="last_step",
    )(x, d, gene, cell)


def exchange(chunks):
    return lax.all_to_all(chunks, "chip", split_axis=0, concat_axis=0, tiled=True)


def swap_cores(chunks):
    return lax.ppermute(chunks, "core", [(0, 1), (1, 0)])


def halo(low):
    n = lax.axis_size("slab")
    before = lax.ppermute(low[CHIPS - 2 * BEFORE :], "slab", [(i, (i + 1) % n) for i in range(n)])
    after = lax.ppermute(low[: 2 * AFTER], "slab", [((i + 1) % n, i) for i in range(n)])
    return before, after


def local(expression, cell_tiles, cell_blocks, cell_counts, gene_tiles, gene_blocks):
    x = expression.T
    cell_at, gene_at = cell_blocks.T, gene_blocks.T
    low = cast_chunks(x)
    mine = exchange(low)
    before, after = halo(low)
    cell = exchange(cell_product(cell_at, cell_counts, before, low, after, cell_tiles, jnp.bfloat16))
    turned = turn_tiles(gene_tiles)
    d, low_rows, rest = first_gene_step(gene_at, turned, mine, swap_cores(mine), cell)
    d_back = exchange(d)
    gene_back = exchange(second_gene_step(gene_at, turned, low_rows, swap_cores(low_rows), rest))
    low = step_chunks(x, d_back)
    before, after = halo(low)
    cell = cell_product(cell_at, cell_counts, before, low, after, cell_tiles, jnp.float32)
    return last_step(x, d_back, gene_back, cell).T


def solution(mesh):
    slabs, inner = mesh.devices.shape
    wide = Mesh(mesh.devices.reshape(slabs, inner // 2, 2), ("slab", "chip", "core"))
    in_specs = (
        P("slab", ("chip", "core")),
        P("slab", None, None, None),
        P("slab", None),
        P("slab"),
        P(),
        P(),
    )
    out_specs = P("slab", ("chip", "core"))
    return jax.shard_map(local, mesh=wide, in_specs=in_specs, out_specs=out_specs, check_vma=False)
```

```python
import jax
import jax.numpy as jnp
from jax import lax
from jax.experimental import pallas as pl
from jax.experimental.pallas import tpu as pltpu
from jax.sharding import Mesh
from jax.sharding import PartitionSpec as P

CHIPS = 32
OWN = 64
CHUNK = 128
BLOCKS = 16
CT = 256
GB = 32
GT = 128
SLOTS = 3
BEFORE, AFTER = 1, 2
HALF = 0.5

VMEM = pl.BlockSpec(memory_space=pltpu.VMEM)
SMEM = pl.BlockSpec(memory_space=pltpu.SMEM)
CHUNKED = (CHIPS, OWN, CHUNK)
DIMS_NT = (((1,), (1,)), ((), ()))


def soft(v):
    return v - jnp.clip(v, -HALF, HALF)


def params(mib):
    return pltpu.CompilerParams(vmem_limit_bytes=mib << 20)


def cost(flops, moved):
    return pl.CostEstimate(flops=flops, bytes_accessed=moved, transcendentals=0)


LOWP_STEP = 4
PART = CHIPS // LOWP_STEP


def low_chunks(values, low_ref, head_ref, tail_ref):
    step = pl.program_id(0)
    low = [values(j).astype(jnp.bfloat16) for j in range(PART)]
    for j in range(PART):
        low_ref[j] = low[j]

    @pl.when(step == 0)
    def _():
        for j in range(2 * AFTER):
            head_ref[j] = low[j]

    @pl.when(step == LOWP_STEP - 1)
    def _():
        for j in range(2 * BEFORE):
            tail_ref[j] = low[PART - 2 * BEFORE + j]


def piece(x_ref, j):
    return x_ref[:, j * CHUNK : (j + 1) * CHUNK]


def cast_kernel(x_ref, low_ref, head_ref, tail_ref):
    low_chunks(lambda j: piece(x_ref, j), low_ref, head_ref, tail_ref)


def move_kernel(x_ref, cell_ref, gene_ref, low_ref, head_ref, tail_ref, d_ref):
    def value(j):
        d = soft(cell_ref[j] + gene_ref[j].astype(jnp.float32))
        d_ref[j] = d
        return piece(x_ref, j) - d

    low_chunks(value, low_ref, head_ref, tail_ref)


X_BLOCK = pl.BlockSpec((OWN, PART * CHUNK), lambda s: (0, s))
PART_BLOCK = pl.BlockSpec((PART, OWN, CHUNK), lambda s: (s, 0, 0))
LOW_SHAPES = [
    jax.ShapeDtypeStruct(CHUNKED, jnp.bfloat16),
    jax.ShapeDtypeStruct((2 * AFTER, OWN, CHUNK), jnp.bfloat16),
    jax.ShapeDtypeStruct((2 * BEFORE, OWN, CHUNK), jnp.bfloat16),
]


def cast_chunks(x):
    return pl.pallas_call(
        cast_kernel,
        grid=(LOWP_STEP,),
        out_shape=LOW_SHAPES,
        in_specs=[X_BLOCK],
        out_specs=[PART_BLOCK, VMEM, VMEM],
        compiler_params=params(8),
        cost_estimate=cost(1 << 18, 3 << 19),
        name="cast_chunks",
    )(x)


def move_chunks(x, cell, gene):
    return pl.pallas_call(
        move_kernel,
        grid=(LOWP_STEP,),
        out_shape=LOW_SHAPES + [jax.ShapeDtypeStruct(CHUNKED, jnp.float32)],
        in_specs=[X_BLOCK, PART_BLOCK, PART_BLOCK],
        out_specs=[PART_BLOCK, VMEM, VMEM, PART_BLOCK],
        compiler_params=params(8),
        cost_estimate=cost(1 << 19, 4 << 20),
        name="move_chunks",
    )(x, cell, gene)


CELL_STEP = 4
CELL_MIB = 48


def cell_blocks_of(refs, tiles_ref, all_ref, put):
    blocks_ref, counts_ref, before_ref, low_ref, after_ref = refs
    step = pl.program_id(0)
    first = lax.axis_index("slab") * BLOCKS - BEFORE

    @pl.when(step == 0)
    def _():
        all_ref[: 2 * BEFORE] = before_ref[...]
        all_ref[2 * BEFORE : 2 * BEFORE + CHIPS] = low_ref[...]
        all_ref[2 * BEFORE + CHIPS :] = after_ref[...]

    for i in range(CELL_STEP):
        b = step * CELL_STEP + i
        total = jnp.zeros((OWN, CT), jnp.float32)
        for k in range(SLOTS):
            at = 2 * (blocks_ref[k, b] - first)
            source = jnp.concatenate([all_ref[at], all_ref[at + 1]], axis=1)
            part = lax.dot_general(source, tiles_ref[i, k], DIMS_NT, preferred_element_type=jnp.float32)
            used = jnp.where(k < counts_ref[b], 1.0, 0.0).astype(jnp.float32)
            total = total + used * part
        put(2 * i, total[:, :CHUNK])
        put(2 * i + 1, total[:, CHUNK:])


def first_cell_kernel(*refs):
    *operands, tiles_ref, out_ref, low_out_ref, all_ref = refs

    def put(j, value):
        out_ref[j] = value
        low_out_ref[j] = value.astype(jnp.bfloat16)

    cell_blocks_of(operands, tiles_ref, all_ref, put)


def second_cell_kernel(*refs):
    *operands, tiles_ref, d_ref, out_ref, all_ref = refs

    def put(j, value):
        out_ref[j] = value + d_ref[j]

    cell_blocks_of(operands, tiles_ref, all_ref, put)


CELL_BLOCK = pl.BlockSpec((2 * CELL_STEP, OWN, CHUNK), lambda s: (s, 0, 0))


def cell_product(kernel, types, operands, tiles, *more):
    return pl.pallas_call(
        kernel,
        grid=(BLOCKS // CELL_STEP,),
        out_shape=[jax.ShapeDtypeStruct(CHUNKED, dtype) for dtype in types],
        in_specs=[
            SMEM,
            SMEM,
            VMEM,
            VMEM,
            VMEM,
            pl.BlockSpec((CELL_STEP, SLOTS, CT, CT), lambda s: (s, 0, 0, 0)),
        ]
        + [CELL_BLOCK] * len(more),
        out_specs=[CELL_BLOCK] * len(types),
        scratch_shapes=[pltpu.VMEM((CHIPS + 2 * (BEFORE + AFTER), OWN, CHUNK), jnp.bfloat16)],
        compiler_params=params(CELL_MIB),
        cost_estimate=cost(2 * BLOCKS * SLOTS * CT * CT * OWN, 9 << 20),
        name="cell_product",
    )(*operands, tiles, *more)


TURN_STEP = 8


def turn_kernel(tiles_ref, out_ref):
    low = lax.axis_index("core") == 0
    for i in range(TURN_STEP):
        for k in range(SLOTS):
            t = tiles_ref[i, k].astype(jnp.float32)
            top, bottom = t[:OWN], t[OWN:]
            mine = jnp.where(low, top, bottom)
            other = jnp.where(low, bottom, top)
            turned = jnp.concatenate([mine, other], axis=0).T
            kept = jnp.where(low, turned[:OWN], turned[OWN:])
            out_ref[i, :, k * GT : (k + 1) * GT] = kept.astype(jnp.bfloat16)


def turn_tiles(gene_tiles):
    return pl.pallas_call(
        turn_kernel,
        grid=(GB // TURN_STEP,),
        out_shape=jax.ShapeDtypeStruct((GB, OWN, SLOTS * GT), jnp.bfloat16),
        in_specs=[pl.BlockSpec((TURN_STEP, SLOTS, GT, GT), lambda s: (s, 0, 0, 0))],
        out_specs=pl.BlockSpec((TURN_STEP, OWN, SLOTS * GT), lambda s: (s, 0, 0)),
        compiler_params=params(8),
        cost_estimate=cost(1 << 24, 5 << 20),
        name="turn_tiles",
    )(gene_tiles)


def gene_block(blocks_ref, turned_ref, mine_ref, other_ref, a):
    parts = []
    for k in range(SLOTS):
        at = blocks_ref[k, a]
        parts += [mine_ref[at], other_ref[at]]
    return jnp.dot(turned_ref[a], jnp.concatenate(parts, axis=0), preferred_element_type=jnp.float32)


GENE_STEP = 16
GENE_BLOCK = pl.BlockSpec((GENE_STEP, OWN, CHUNK), lambda s: (s, 0, 0))


def first_gene_kernel(blocks_ref, turned_ref, mine_ref, other_ref, sent_ref, gene_ref):
    for i in range(GENE_STEP):
        a = pl.program_id(0) * GENE_STEP + i
        gene = gene_block(blocks_ref, turned_ref, mine_ref, other_ref, a)
        sent_ref[i] = gene.astype(jnp.bfloat16)
        gene_ref[i] = gene


def first_gene(blocks, turned, mine, other):
    return pl.pallas_call(
        first_gene_kernel,
        grid=(GB // GENE_STEP,),
        out_shape=[jax.ShapeDtypeStruct(CHUNKED, jnp.bfloat16), jax.ShapeDtypeStruct(CHUNKED, jnp.float32)],
        in_specs=[SMEM, VMEM, VMEM, VMEM],
        out_specs=[GENE_BLOCK, GENE_BLOCK],
        compiler_params=params(16),
        cost_estimate=cost(2 * GB * OWN * SLOTS * GT * CHUNK, 5 << 20),
        name="first_gene",
    )(blocks, turned, mine, other)


def rows_kernel(mine_ref, gene_ref, cell_ref, low_ref, rest_ref):
    for i in range(GENE_STEP):
        gene, cell = gene_ref[i], cell_ref[i].astype(jnp.float32)
        d = soft(cell + gene)
        rest_ref[i] = d - soft(cell + gene.astype(jnp.bfloat16).astype(jnp.float32))
        low_ref[i] = (mine_ref[i].astype(jnp.float32) - d).astype(jnp.bfloat16)


def move_rows(mine, gene, cell):
    return pl.pallas_call(
        rows_kernel,
        grid=(GB // GENE_STEP,),
        out_shape=[jax.ShapeDtypeStruct(CHUNKED, jnp.bfloat16), jax.ShapeDtypeStruct(CHUNKED, jnp.float32)],
        in_specs=[GENE_BLOCK] * 3,
        out_specs=[GENE_BLOCK] * 2,
        compiler_params=params(16),
        cost_estimate=cost(1 << 20, 4 << 20),
        name="move_rows",
    )(mine, gene, cell)


def second_gene_kernel(blocks_ref, turned_ref, mine_ref, other_ref, rest_ref, out_ref):
    for i in range(GENE_STEP):
        a = pl.program_id(0) * GENE_STEP + i
        gene = gene_block(blocks_ref, turned_ref, mine_ref, other_ref, a)
        out_ref[i] = (gene + rest_ref[i]).astype(jnp.bfloat16)


def second_gene(blocks, turned, mine, other, rest):
    return pl.pallas_call(
        second_gene_kernel,
        grid=(GB // GENE_STEP,),
        out_shape=jax.ShapeDtypeStruct(CHUNKED, jnp.bfloat16),
        in_specs=[SMEM, VMEM, VMEM, VMEM, GENE_BLOCK],
        out_specs=GENE_BLOCK,
        compiler_params=params(16),
        cost_estimate=cost(2 * GB * OWN * SLOTS * GT * CHUNK, 5 << 20),
        name="second_gene",
    )(blocks, turned, mine, other, rest)


def last_kernel(x_ref, near_ref, gene_ref, out_ref):
    for j in range(PART):
        at = slice(j * CHUNK, (j + 1) * CHUNK)
        out_ref[:, at] = piece(x_ref, j) - soft(near_ref[j] + gene_ref[j].astype(jnp.float32))


def last_step(x, near, gene):
    return pl.pallas_call(
        last_kernel,
        grid=(LOWP_STEP,),
        out_shape=jax.ShapeDtypeStruct(x.shape, jnp.float32),
        in_specs=[X_BLOCK, PART_BLOCK, PART_BLOCK],
        out_specs=X_BLOCK,
        compiler_params=params(12),
        cost_estimate=cost(1 << 20, 4 << 20),
        name="last_step",
    )(x, near, gene)


def exchange(chunks):
    return lax.all_to_all(chunks, "chip", split_axis=0, concat_axis=0, tiled=True)


def swap_cores(chunks):
    return lax.ppermute(chunks, "core", [(0, 1), (1, 0)])


def halo(head, tail):
    n = lax.axis_size("slab")
    before = lax.ppermute(tail, "slab", [(i, (i + 1) % n) for i in range(n)])
    after = lax.ppermute(head, "slab", [((i + 1) % n, i) for i in range(n)])
    return before, after


def local(expression, cell_tiles, cell_blocks, cell_counts, gene_tiles, gene_blocks):
    x = expression.T
    cell_at, gene_at = cell_blocks.T, gene_blocks.T
    low, head, tail = cast_chunks(x)
    mine = exchange(low)
    before, after = halo(head, tail)
    f32, bf16 = jnp.float32, jnp.bfloat16
    operands = (cell_at, cell_counts, before, low, after)
    cell, cell_sent = cell_product(first_cell_kernel, (f32, bf16), operands, cell_tiles)
    cell_rows = exchange(cell_sent)
    turned = turn_tiles(gene_tiles)
    gene_sent, gene_rows = first_gene(gene_at, turned, mine, swap_cores(mine))
    gene = exchange(gene_sent)
    low_rows, rest = move_rows(mine, gene_rows, cell_rows)
    gene_last = exchange(second_gene(gene_at, turned, low_rows, swap_cores(low_rows), rest))
    low, head, tail, d = move_chunks(x, cell, gene)
    before, after = halo(head, tail)
    operands = (cell_at, cell_counts, before, low, after)
    (near,) = cell_product(second_cell_kernel, (f32,), operands, cell_tiles, d)
    return last_step(x, near, gene_last).T


def solution(mesh):
    slabs, inner = mesh.devices.shape
    wide = Mesh(mesh.devices.reshape(slabs, inner // 2, 2), ("slab", "chip", "core"))
    in_specs = (
        P("slab", ("chip", "core")),
        P("slab", None, None, None),
        P("slab", None),
        P("slab"),
        P(),
        P(),
    )
    out_specs = P("slab", ("chip", "core"))
    return jax.shard_map(local, mesh=wide, in_specs=in_specs, out_specs=out_specs, check_vma=False)
```

```python
import jax
import jax.numpy as jnp
from jax import lax
from jax.experimental import pallas as pl
from jax.experimental.pallas import tpu as pltpu
from jax.sharding import Mesh
from jax.sharding import PartitionSpec as P

CHIPS = 32
OWN = 64
CHUNK = 128
BLOCKS = 16
CT = 256
GB = 32
GT = 128
SLOTS = 3
BEFORE, AFTER = 1, 2
HALF = 0.5

VMEM = pl.BlockSpec(memory_space=pltpu.VMEM)
SMEM = pl.BlockSpec(memory_space=pltpu.SMEM)
CHUNKED = (CHIPS, OWN, CHUNK)
DIMS_NT = (((1,), (1,)), ((), ()))


def soft(v):
    return v - jnp.clip(v, -HALF, HALF)


def params(mib):
    return pltpu.CompilerParams(vmem_limit_bytes=mib << 20)


def cost(flops, moved):
    return pl.CostEstimate(flops=flops, bytes_accessed=moved, transcendentals=0)


LOWP_STEP = 4
PART = CHIPS // LOWP_STEP


def low_chunks(values, low_ref, head_ref, tail_ref):
    step = pl.program_id(0)
    low = [values(j).astype(jnp.bfloat16) for j in range(PART)]
    for j in range(PART):
        low_ref[j] = low[j]

    @pl.when(step == 0)
    def _():
        for j in range(2 * AFTER):
            head_ref[j] = low[j]

    @pl.when(step == LOWP_STEP - 1)
    def _():
        for j in range(2 * BEFORE):
            tail_ref[j] = low[PART - 2 * BEFORE + j]


def piece(x_ref, j):
    return x_ref[:, j * CHUNK : (j + 1) * CHUNK]


def cast_kernel(x_ref, low_ref, head_ref, tail_ref):
    low_chunks(lambda j: piece(x_ref, j), low_ref, head_ref, tail_ref)


def move_kernel(x_ref, cell_ref, gene_ref, low_ref, head_ref, tail_ref, d_ref):
    def value(j):
        d = soft(cell_ref[j] + gene_ref[j].astype(jnp.float32))
        d_ref[j] = d
        return piece(x_ref, j) - d

    low_chunks(value, low_ref, head_ref, tail_ref)


X_BLOCK = pl.BlockSpec((OWN, PART * CHUNK), lambda s: (0, s))
PART_BLOCK = pl.BlockSpec((PART, OWN, CHUNK), lambda s: (s, 0, 0))
LOW_SHAPES = [
    jax.ShapeDtypeStruct(CHUNKED, jnp.bfloat16),
    jax.ShapeDtypeStruct((2 * AFTER, OWN, CHUNK), jnp.bfloat16),
    jax.ShapeDtypeStruct((2 * BEFORE, OWN, CHUNK), jnp.bfloat16),
]


def cast_chunks(x):
    return pl.pallas_call(
        cast_kernel,
        grid=(LOWP_STEP,),
        out_shape=LOW_SHAPES,
        in_specs=[X_BLOCK],
        out_specs=[PART_BLOCK, VMEM, VMEM],
        compiler_params=params(8),
        cost_estimate=cost(1 << 18, 3 << 19),
        name="cast_chunks",
    )(x)


def move_chunks(x, cell, gene):
    return pl.pallas_call(
        move_kernel,
        grid=(LOWP_STEP,),
        out_shape=LOW_SHAPES + [jax.ShapeDtypeStruct(CHUNKED, jnp.float32)],
        in_specs=[X_BLOCK, PART_BLOCK, PART_BLOCK],
        out_specs=[PART_BLOCK, VMEM, VMEM, PART_BLOCK],
        compiler_params=params(8),
        cost_estimate=cost(1 << 19, 4 << 20),
        name="move_chunks",
    )(x, cell, gene)


CELL_STEP = 4
CELL_MIB = 48


def cell_blocks_of(refs, tiles_ref, all_ref, put):
    blocks_ref, counts_ref, before_ref, low_ref, after_ref = refs
    step = pl.program_id(0)
    first = lax.axis_index("slab") * BLOCKS - BEFORE

    @pl.when(step == 0)
    def _():
        all_ref[: 2 * BEFORE] = before_ref[...]
        all_ref[2 * BEFORE : 2 * BEFORE + CHIPS] = low_ref[...]
        all_ref[2 * BEFORE + CHIPS :] = after_ref[...]

    for i in range(CELL_STEP):
        b = step * CELL_STEP + i
        total = jnp.zeros((OWN, CT), jnp.float32)
        for k in range(SLOTS):
            at = 2 * (blocks_ref[k, b] - first)
            source = jnp.concatenate([all_ref[at], all_ref[at + 1]], axis=1)
            part = lax.dot_general(source, tiles_ref[i, k], DIMS_NT, preferred_element_type=jnp.float32)
            used = jnp.where(k < counts_ref[b], 1.0, 0.0).astype(jnp.float32)
            total = total + used * part
        put(2 * i, total[:, :CHUNK])
        put(2 * i + 1, total[:, CHUNK:])


def first_cell_kernel(*refs):
    *operands, tiles_ref, out_ref, low_out_ref, all_ref = refs

    def put(j, value):
        out_ref[j] = value
        low_out_ref[j] = value.astype(jnp.bfloat16)

    cell_blocks_of(operands, tiles_ref, all_ref, put)


def second_cell_kernel(*refs):
    *operands, tiles_ref, d_ref, out_ref, all_ref = refs

    def put(j, value):
        out_ref[j] = value + d_ref[j]

    cell_blocks_of(operands, tiles_ref, all_ref, put)


CELL_BLOCK = pl.BlockSpec((2 * CELL_STEP, OWN, CHUNK), lambda s: (s, 0, 0))


def cell_product(kernel, types, operands, tiles, *more):
    return pl.pallas_call(
        kernel,
        grid=(BLOCKS // CELL_STEP,),
        out_shape=[jax.ShapeDtypeStruct(CHUNKED, dtype) for dtype in types],
        in_specs=[
            SMEM,
            SMEM,
            VMEM,
            VMEM,
            VMEM,
            pl.BlockSpec((CELL_STEP, SLOTS, CT, CT), lambda s: (s, 0, 0, 0)),
        ]
        + [CELL_BLOCK] * len(more),
        out_specs=[CELL_BLOCK] * len(types),
        scratch_shapes=[pltpu.VMEM((CHIPS + 2 * (BEFORE + AFTER), OWN, CHUNK), jnp.bfloat16)],
        compiler_params=params(CELL_MIB),
        cost_estimate=cost(2 * BLOCKS * SLOTS * CT * CT * OWN, 9 << 20),
        name="cell_product",
    )(*operands, tiles, *more)


TURN_STEP = 8


def turn_kernel(tiles_ref, out_ref):
    low = lax.axis_index("core") == 0
    for i in range(TURN_STEP):
        for k in range(SLOTS):
            t = tiles_ref[i, k].astype(jnp.float32)
            top, bottom = t[:OWN], t[OWN:]
            mine = jnp.where(low, top, bottom)
            other = jnp.where(low, bottom, top)
            turned = jnp.concatenate([mine, other], axis=0).T
            kept = jnp.where(low, turned[:OWN], turned[OWN:])
            out_ref[i, :, k * GT : (k + 1) * GT] = kept.astype(jnp.bfloat16)


def turn_tiles(gene_tiles):
    return pl.pallas_call(
        turn_kernel,
        grid=(GB // TURN_STEP,),
        out_shape=jax.ShapeDtypeStruct((GB, OWN, SLOTS * GT), jnp.bfloat16),
        in_specs=[pl.BlockSpec((TURN_STEP, SLOTS, GT, GT), lambda s: (s, 0, 0, 0))],
        out_specs=pl.BlockSpec((TURN_STEP, OWN, SLOTS * GT), lambda s: (s, 0, 0)),
        compiler_params=params(8),
        cost_estimate=cost(1 << 24, 5 << 20),
        name="turn_tiles",
    )(gene_tiles)


def gene_block(blocks_ref, turned_ref, mine_ref, other_ref, a):
    parts = []
    for k in range(SLOTS):
        at = blocks_ref[k, a]
        parts += [mine_ref[at], other_ref[at]]
    return jnp.dot(turned_ref[a], jnp.concatenate(parts, axis=0), preferred_element_type=jnp.float32)


GENE_STEP = 16
GENE_BLOCK = pl.BlockSpec((GENE_STEP, OWN, CHUNK), lambda s: (s, 0, 0))


def first_gene_kernel(blocks_ref, turned_ref, mine_ref, other_ref, sent_ref, gene_ref):
    for i in range(GENE_STEP):
        a = pl.program_id(0) * GENE_STEP + i
        gene = gene_block(blocks_ref, turned_ref, mine_ref, other_ref, a)
        sent_ref[i] = gene.astype(jnp.bfloat16)
        gene_ref[i] = gene


def first_gene(blocks, turned, mine, other):
    return pl.pallas_call(
        first_gene_kernel,
        grid=(GB // GENE_STEP,),
        out_shape=[jax.ShapeDtypeStruct(CHUNKED, jnp.bfloat16), jax.ShapeDtypeStruct(CHUNKED, jnp.float32)],
        in_specs=[SMEM, VMEM, VMEM, VMEM],
        out_specs=[GENE_BLOCK, GENE_BLOCK],
        compiler_params=params(16),
        cost_estimate=cost(2 * GB * OWN * SLOTS * GT * CHUNK, 5 << 20),
        name="first_gene",
    )(blocks, turned, mine, other)


def rows_kernel(mine_ref, gene_ref, cell_ref, low_ref, rest_ref):
    for i in range(GENE_STEP):
        gene, cell = gene_ref[i], cell_ref[i].astype(jnp.float32)
        d = soft(cell + gene)
        rest_ref[i] = d - soft(cell + gene.astype(jnp.bfloat16).astype(jnp.float32))
        low_ref[i] = (mine_ref[i].astype(jnp.float32) - d).astype(jnp.bfloat16)


def move_rows(mine, gene, cell):
    return pl.pallas_call(
        rows_kernel,
        grid=(GB // GENE_STEP,),
        out_shape=[jax.ShapeDtypeStruct(CHUNKED, jnp.bfloat16), jax.ShapeDtypeStruct(CHUNKED, jnp.float32)],
        in_specs=[GENE_BLOCK] * 3,
        out_specs=[GENE_BLOCK] * 2,
        compiler_params=params(16),
        cost_estimate=cost(1 << 20, 4 << 20),
        name="move_rows",
    )(mine, gene, cell)


def second_gene_kernel(blocks_ref, turned_ref, mine_ref, other_ref, rest_ref, out_ref):
    for i in range(GENE_STEP):
        a = pl.program_id(0) * GENE_STEP + i
        gene = gene_block(blocks_ref, turned_ref, mine_ref, other_ref, a)
        out_ref[i] = (gene + rest_ref[i]).astype(jnp.bfloat16)


def second_gene(blocks, turned, mine, other, rest):
    return pl.pallas_call(
        second_gene_kernel,
        grid=(GB // GENE_STEP,),
        out_shape=jax.ShapeDtypeStruct(CHUNKED, jnp.bfloat16),
        in_specs=[SMEM, VMEM, VMEM, VMEM, GENE_BLOCK],
        out_specs=GENE_BLOCK,
        compiler_params=params(16),
        cost_estimate=cost(2 * GB * OWN * SLOTS * GT * CHUNK, 5 << 20),
        name="second_gene",
    )(blocks, turned, mine, other, rest)


def last_kernel(x_ref, near_ref, gene_ref, out_ref, ready_ref, sems):
    copies = []
    for s in range(LOWP_STEP):
        at = slice(s * PART * CHUNK, (s + 1) * PART * CHUNK)
        for j in range(s * PART, (s + 1) * PART):
            v = near_ref[j] + gene_ref[j].astype(jnp.float32)
            ready_ref[:, j * CHUNK : (j + 1) * CHUNK] = piece(x_ref, j) - soft(v)
        copy = pltpu.make_async_copy(ready_ref.at[:, at], out_ref.at[:, at], sems.at[s])
        copy.start()
        copies.append(copy)
    for copy in copies:
        copy.wait()


def last_step(x, near, gene):
    return pl.pallas_call(
        last_kernel,
        out_shape=jax.ShapeDtypeStruct(x.shape, jnp.float32),
        in_specs=[VMEM] * 3,
        out_specs=pl.BlockSpec(memory_space=pl.ANY),
        scratch_shapes=[pltpu.VMEM((OWN, CHIPS * CHUNK), jnp.float32), pltpu.SemaphoreType.DMA((LOWP_STEP,))],
        compiler_params=params(8),
        cost_estimate=cost(1 << 20, 4 << 20),
        name="last_step",
    )(x, near, gene)


def exchange(chunks):
    return lax.all_to_all(chunks, "chip", split_axis=0, concat_axis=0, tiled=True)


def swap_cores(chunks):
    return lax.ppermute(chunks, "core", [(0, 1), (1, 0)])


def halo(head, tail):
    n = lax.axis_size("slab")
    before = lax.ppermute(tail, "slab", [(i, (i + 1) % n) for i in range(n)])
    after = lax.ppermute(head, "slab", [((i + 1) % n, i) for i in range(n)])
    return before, after


def local(expression, cell_tiles, cell_blocks, cell_counts, gene_tiles, gene_blocks):
    x = expression.T
    cell_at, gene_at = cell_blocks.T, gene_blocks.T
    low, head, tail = cast_chunks(x)
    mine = exchange(low)
    before, after = halo(head, tail)
    f32, bf16 = jnp.float32, jnp.bfloat16
    operands = (cell_at, cell_counts, before, low, after)
    cell, cell_sent = cell_product(first_cell_kernel, (f32, bf16), operands, cell_tiles)
    cell_rows = exchange(cell_sent)
    turned = turn_tiles(gene_tiles)
    gene_sent, gene_rows = first_gene(gene_at, turned, mine, swap_cores(mine))
    gene = exchange(gene_sent)
    low_rows, rest = move_rows(mine, gene_rows, cell_rows)
    gene_last = exchange(second_gene(gene_at, turned, low_rows, swap_cores(low_rows), rest))
    low, head, tail, d = move_chunks(x, cell, gene)
    before, after = halo(head, tail)
    operands = (cell_at, cell_counts, before, low, after)
    (near,) = cell_product(second_cell_kernel, (f32,), operands, cell_tiles, d)
    return last_step(x, near, gene_last).T


def solution(mesh):
    slabs, inner = mesh.devices.shape
    wide = Mesh(mesh.devices.reshape(slabs, inner // 2, 2), ("slab", "chip", "core"))
    in_specs = (
        P("slab", ("chip", "core")),
        P("slab", None, None, None),
        P("slab", None),
        P("slab"),
        P(),
        P(),
    )
    out_specs = P("slab", ("chip", "core"))
    return jax.shard_map(local, mesh=wide, in_specs=in_specs, out_specs=out_specs, check_vma=False)
```

```python
import jax
import jax.numpy as jnp
from jax import lax
from jax.experimental import pallas as pl
from jax.experimental.pallas import tpu as pltpu
from jax.sharding import Mesh
from jax.sharding import PartitionSpec as P

CHIPS = 32
OWN = 64
CHUNK = 128
BLOCKS = 16
CT = 256
GB = 32
GT = 128
SLOTS = 3
BEFORE, AFTER = 1, 2
HALF = 0.5

VMEM = pl.BlockSpec(memory_space=pltpu.VMEM)
SMEM = pl.BlockSpec(memory_space=pltpu.SMEM)
HBM = pl.BlockSpec(memory_space=pl.ANY)
CHUNKED = (CHIPS, OWN, CHUNK)
DIMS_NT = (((1,), (1,)), ((), ()))


def soft(v):
    return v - jnp.clip(v, -HALF, HALF)


def params(mib):
    return pltpu.CompilerParams(vmem_limit_bytes=mib << 20)


def cost(flops, moved):
    return pl.CostEstimate(flops=flops, bytes_accessed=moved, transcendentals=0)


LOWP_STEP = 4
PART = CHIPS // LOWP_STEP


def low_chunks(values, low_ref, head_ref, tail_ref):
    step = pl.program_id(0)
    low = [values(j).astype(jnp.bfloat16) for j in range(PART)]
    for j in range(PART):
        low_ref[j] = low[j]

    @pl.when(step == 0)
    def _():
        for j in range(2 * AFTER):
            head_ref[j] = low[j]

    @pl.when(step == LOWP_STEP - 1)
    def _():
        for j in range(2 * BEFORE):
            tail_ref[j] = low[PART - 2 * BEFORE + j]


def piece(x_ref, j):
    return x_ref[:, j * CHUNK : (j + 1) * CHUNK]


def cast_kernel(x_ref, low_ref, head_ref, tail_ref, x_held, low_held, in_sems, out_sems):
    width = PART * CHUNK
    fetches = [
        pltpu.make_async_copy(x_ref.at[:, pl.ds(s * width, width)], x_held.at[:, pl.ds(s * width, width)], in_sems.at[s])
        for s in range(LOWP_STEP)
    ]
    for copy in fetches:
        copy.start()
    sends = []
    for s in range(LOWP_STEP):
        fetches[s].wait()
        for j in range(s * PART, (s + 1) * PART):
            low_held[j] = piece(x_held, j).astype(jnp.bfloat16)
        at = pl.ds(s * PART, PART)
        send = pltpu.make_async_copy(low_held.at[at], low_ref.at[at], out_sems.at[s])
        send.start()
        sends.append(send)
    head_ref[...] = low_held[: 2 * AFTER]
    tail_ref[...] = low_held[CHIPS - 2 * BEFORE :]
    for send in sends:
        send.wait()


def move_kernel(x_ref, cell_ref, gene_ref, low_ref, head_ref, tail_ref, d_ref):
    def value(j):
        d = soft(cell_ref[j] + gene_ref[j].astype(jnp.float32))
        d_ref[j] = d
        return piece(x_ref, j) - d

    low_chunks(value, low_ref, head_ref, tail_ref)


X_BLOCK = pl.BlockSpec((OWN, PART * CHUNK), lambda s: (0, s))
PART_BLOCK = pl.BlockSpec((PART, OWN, CHUNK), lambda s: (s, 0, 0))
LOW_SHAPES = [
    jax.ShapeDtypeStruct(CHUNKED, jnp.bfloat16),
    jax.ShapeDtypeStruct((2 * AFTER, OWN, CHUNK), jnp.bfloat16),
    jax.ShapeDtypeStruct((2 * BEFORE, OWN, CHUNK), jnp.bfloat16),
]


def cast_chunks(x):
    return pl.pallas_call(
        cast_kernel,
        out_shape=LOW_SHAPES,
        in_specs=[HBM],
        out_specs=[HBM, VMEM, VMEM],
        scratch_shapes=[
            pltpu.VMEM((OWN, CHIPS * CHUNK), jnp.float32),
            pltpu.VMEM(CHUNKED, jnp.bfloat16),
            pltpu.SemaphoreType.DMA((LOWP_STEP,)),
            pltpu.SemaphoreType.DMA((LOWP_STEP,)),
        ],
        compiler_params=params(60),
        cost_estimate=cost(1 << 18, 3 << 19),
        name="cast_chunks",
    )(x)


def move_chunks(x, cell, gene):
    return pl.pallas_call(
        move_kernel,
        grid=(LOWP_STEP,),
        out_shape=LOW_SHAPES + [jax.ShapeDtypeStruct(CHUNKED, jnp.float32)],
        in_specs=[X_BLOCK, PART_BLOCK, PART_BLOCK],
        out_specs=[PART_BLOCK, VMEM, VMEM, PART_BLOCK],
        compiler_params=params(8),
        cost_estimate=cost(1 << 19, 4 << 20),
        name="move_chunks",
    )(x, cell, gene)


CELL_STEP = 8
CELL_MIB = 48


def cell_blocks_of(refs, tiles_ref, all_ref, put):
    blocks_ref, counts_ref, before_ref, low_ref, after_ref = refs
    step = pl.program_id(0)
    first = lax.axis_index("slab") * BLOCKS - BEFORE

    @pl.when(step == 0)
    def _():
        all_ref[: 2 * BEFORE] = before_ref[...]
        all_ref[2 * BEFORE : 2 * BEFORE + CHIPS] = low_ref[...]
        all_ref[2 * BEFORE + CHIPS :] = after_ref[...]

    for i in range(CELL_STEP):
        b = step * CELL_STEP + i
        total = jnp.zeros((OWN, CT), jnp.float32)
        for k in range(SLOTS):
            at = 2 * (blocks_ref[k, b] - first)
            source = jnp.concatenate([all_ref[at], all_ref[at + 1]], axis=1)
            part = lax.dot_general(source, tiles_ref[i, k], DIMS_NT, preferred_element_type=jnp.float32)
            used = jnp.where(k < counts_ref[b], 1.0, 0.0).astype(jnp.float32)
            total = total + used * part
        put(2 * i, total[:, :CHUNK])
        put(2 * i + 1, total[:, CHUNK:])


def first_cell_kernel(*refs):
    *operands, tiles_ref, out_ref, low_out_ref, all_ref = refs

    def put(j, value):
        out_ref[j] = value
        low_out_ref[j] = value.astype(jnp.bfloat16)

    cell_blocks_of(operands, tiles_ref, all_ref, put)


def second_cell_kernel(*refs):
    *operands, tiles_ref, d_ref, out_ref, all_ref = refs

    def put(j, value):
        out_ref[j] = value + d_ref[j]

    cell_blocks_of(operands, tiles_ref, all_ref, put)


CELL_BLOCK = pl.BlockSpec((2 * CELL_STEP, OWN, CHUNK), lambda s: (s, 0, 0))


def cell_product(kernel, types, operands, tiles, *more):
    return pl.pallas_call(
        kernel,
        grid=(BLOCKS // CELL_STEP,),
        out_shape=[jax.ShapeDtypeStruct(CHUNKED, dtype) for dtype in types],
        in_specs=[
            SMEM,
            SMEM,
            VMEM,
            VMEM,
            VMEM,
            pl.BlockSpec((CELL_STEP, SLOTS, CT, CT), lambda s: (s, 0, 0, 0)),
        ]
        + [CELL_BLOCK] * len(more),
        out_specs=[CELL_BLOCK] * len(types),
        scratch_shapes=[pltpu.VMEM((CHIPS + 2 * (BEFORE + AFTER), OWN, CHUNK), jnp.bfloat16)],
        compiler_params=params(CELL_MIB),
        cost_estimate=cost(2 * BLOCKS * SLOTS * CT * CT * OWN, 9 << 20),
        name="cell_product",
    )(*operands, tiles, *more)


TURN_STEP = 8


def turn_kernel(tiles_ref, out_ref):
    low = lax.axis_index("core") == 0
    for i in range(TURN_STEP):
        for k in range(SLOTS):
            t = tiles_ref[i, k].astype(jnp.float32)
            top, bottom = t[:OWN], t[OWN:]
            mine = jnp.where(low, top, bottom)
            other = jnp.where(low, bottom, top)
            turned = jnp.concatenate([mine, other], axis=0).T
            kept = jnp.where(low, turned[:OWN], turned[OWN:])
            out_ref[i, :, k * GT : (k + 1) * GT] = kept.astype(jnp.bfloat16)


def turn_tiles(gene_tiles):
    return pl.pallas_call(
        turn_kernel,
        grid=(GB // TURN_STEP,),
        out_shape=jax.ShapeDtypeStruct((GB, OWN, SLOTS * GT), jnp.bfloat16),
        in_specs=[pl.BlockSpec((TURN_STEP, SLOTS, GT, GT), lambda s: (s, 0, 0, 0))],
        out_specs=pl.BlockSpec((TURN_STEP, OWN, SLOTS * GT), lambda s: (s, 0, 0)),
        compiler_params=params(8),
        cost_estimate=cost(1 << 24, 5 << 20),
        name="turn_tiles",
    )(gene_tiles)


def gene_block(blocks_ref, turned_ref, mine_ref, other_ref, a):
    parts = []
    for k in range(SLOTS):
        at = blocks_ref[k, a]
        parts += [mine_ref[at], other_ref[at]]
    return jnp.dot(turned_ref[a], jnp.concatenate(parts, axis=0), preferred_element_type=jnp.float32)


GENE_STEP = 16
GENE_BLOCK = pl.BlockSpec((GENE_STEP, OWN, CHUNK), lambda s: (s, 0, 0))


def first_gene_kernel(blocks_ref, turned_ref, mine_ref, other_ref, sent_ref, gene_ref):
    for i in range(GENE_STEP):
        a = pl.program_id(0) * GENE_STEP + i
        gene = gene_block(blocks_ref, turned_ref, mine_ref, other_ref, a)
        sent_ref[i] = gene.astype(jnp.bfloat16)
        gene_ref[i] = gene


def first_gene(blocks, turned, mine, other):
    return pl.pallas_call(
        first_gene_kernel,
        grid=(GB // GENE_STEP,),
        out_shape=[jax.ShapeDtypeStruct(CHUNKED, jnp.bfloat16), jax.ShapeDtypeStruct(CHUNKED, jnp.float32)],
        in_specs=[SMEM, VMEM, VMEM, VMEM],
        out_specs=[GENE_BLOCK, GENE_BLOCK],
        compiler_params=params(16),
        cost_estimate=cost(2 * GB * OWN * SLOTS * GT * CHUNK, 5 << 20),
        name="first_gene",
    )(blocks, turned, mine, other)


def rows_kernel(mine_ref, gene_ref, cell_ref, low_ref, rest_ref):
    for i in range(GENE_STEP):
        gene, cell = gene_ref[i], cell_ref[i].astype(jnp.float32)
        d = soft(cell + gene)
        rest_ref[i] = d - soft(cell + gene.astype(jnp.bfloat16).astype(jnp.float32))
        low_ref[i] = (mine_ref[i].astype(jnp.float32) - d).astype(jnp.bfloat16)


def move_rows(mine, gene, cell):
    return pl.pallas_call(
        rows_kernel,
        grid=(GB // GENE_STEP,),
        out_shape=[jax.ShapeDtypeStruct(CHUNKED, jnp.bfloat16), jax.ShapeDtypeStruct(CHUNKED, jnp.float32)],
        in_specs=[GENE_BLOCK] * 3,
        out_specs=[GENE_BLOCK] * 2,
        compiler_params=params(16),
        cost_estimate=cost(1 << 20, 4 << 20),
        name="move_rows",
    )(mine, gene, cell)


def second_gene_kernel(blocks_ref, turned_ref, mine_ref, other_ref, rest_ref, out_ref):
    for i in range(GENE_STEP):
        a = pl.program_id(0) * GENE_STEP + i
        gene = gene_block(blocks_ref, turned_ref, mine_ref, other_ref, a)
        out_ref[i] = (gene + rest_ref[i]).astype(jnp.bfloat16)


def second_gene(blocks, turned, mine, other, rest):
    return pl.pallas_call(
        second_gene_kernel,
        grid=(GB // GENE_STEP,),
        out_shape=jax.ShapeDtypeStruct(CHUNKED, jnp.bfloat16),
        in_specs=[SMEM, VMEM, VMEM, VMEM, GENE_BLOCK],
        out_specs=GENE_BLOCK,
        compiler_params=params(16),
        cost_estimate=cost(2 * GB * OWN * SLOTS * GT * CHUNK, 5 << 20),
        name="second_gene",
    )(blocks, turned, mine, other, rest)


def last_kernel(x_ref, near_ref, gene_ref, out_ref, ready_ref, sems):
    copies = []
    for s in range(LOWP_STEP):
        at = slice(s * PART * CHUNK, (s + 1) * PART * CHUNK)
        for j in range(s * PART, (s + 1) * PART):
            v = near_ref[j] + gene_ref[j].astype(jnp.float32)
            ready_ref[:, j * CHUNK : (j + 1) * CHUNK] = piece(x_ref, j) - soft(v)
        copy = pltpu.make_async_copy(ready_ref.at[:, at], out_ref.at[:, at], sems.at[s])
        copy.start()
        copies.append(copy)
    for copy in copies:
        copy.wait()


def last_step(x, near, gene):
    return pl.pallas_call(
        last_kernel,
        out_shape=jax.ShapeDtypeStruct(x.shape, jnp.float32),
        in_specs=[VMEM] * 3,
        out_specs=pl.BlockSpec(memory_space=pl.ANY),
        scratch_shapes=[pltpu.VMEM((OWN, CHIPS * CHUNK), jnp.float32), pltpu.SemaphoreType.DMA((LOWP_STEP,))],
        compiler_params=params(8),
        cost_estimate=cost(1 << 20, 4 << 20),
        name="last_step",
    )(x, near, gene)


def exchange(chunks):
    return lax.all_to_all(chunks, "chip", split_axis=0, concat_axis=0, tiled=True)


def swap_cores(chunks):
    return lax.ppermute(chunks, "core", [(0, 1), (1, 0)])


def halo(head, tail):
    n = lax.axis_size("slab")
    before = lax.ppermute(tail, "slab", [(i, (i + 1) % n) for i in range(n)])
    after = lax.ppermute(head, "slab", [((i + 1) % n, i) for i in range(n)])
    return before, after


def local(expression, cell_tiles, cell_blocks, cell_counts, gene_tiles, gene_blocks):
    x = expression.T
    cell_at, gene_at = cell_blocks.T, gene_blocks.T
    low, head, tail = cast_chunks(x)
    mine = exchange(low)
    before, after = halo(head, tail)
    f32, bf16 = jnp.float32, jnp.bfloat16
    operands = (cell_at, cell_counts, before, low, after)
    cell, cell_sent = cell_product(first_cell_kernel, (f32, bf16), operands, cell_tiles)
    cell_rows = exchange(cell_sent)
    turned = turn_tiles(gene_tiles)
    gene_sent, gene_rows = first_gene(gene_at, turned, mine, swap_cores(mine))
    gene = exchange(gene_sent)
    low_rows, rest = move_rows(mine, gene_rows, cell_rows)
    gene_last = exchange(second_gene(gene_at, turned, low_rows, swap_cores(low_rows), rest))
    low, head, tail, d = move_chunks(x, cell, gene)
    before, after = halo(head, tail)
    operands = (cell_at, cell_counts, before, low, after)
    (near,) = cell_product(second_cell_kernel, (f32,), operands, cell_tiles, d)
    return last_step(x, near, gene_last).T


def solution(mesh):
    slabs, inner = mesh.devices.shape
    wide = Mesh(mesh.devices.reshape(slabs, inner // 2, 2), ("slab", "chip", "core"))
    in_specs = (
        P("slab", ("chip", "core")),
        P("slab", None, None, None),
        P("slab", None),
        P("slab"),
        P(),
        P(),
    )
    out_specs = P("slab", ("chip", "core"))
    return jax.shard_map(local, mesh=wide, in_specs=in_specs, out_specs=out_specs, check_vma=False)
```
